1024 devices in a mesh: expert: 32 (over z, core), col: 8 (over y), dp: 4 (over x).
Axes of the slice: x: 4, y: 8, z: 16, core: 2. Of those that a mesh axis runs over, the one named last changes fastest.
Arguments:
- tokens: bfloat16 [16384, 8192], P(('expert', 'dp'), 'col'), may hold values from -6 to 6
- cotangent: bfloat16 [16384, 8192], P(('expert', 'dp'), 'col'), may hold values from -6 to 6
- expert_ids: int32 [16384, 4], P(('expert', 'dp')), may hold values from 0 to 63, all different within a row; in each aligned block of 128 rows (0 to 127, 128 to 255, ...) at most 10 rows name the same one
- gate_codes: int32 [16384, 4], P(('expert', 'dp')), may hold values from 1 to 255
- w_in: bfloat16 [64, 8192, 448], P('expert', 'col'), may hold values from -0.0625 to 0.0625
- w_out: bfloat16 [64, 224, 8192], P('expert', None, 'col'), may hold values from -0.375 to 0.375
Outputs:
- grad_tokens: bfloat16 [16384, 8192], P(('expert', 'dp'), 'col')
- grad_in: float32 [64, 8192, 448], P('expert', ('col', 'dp'))
The draws below stay inside these ranges and needn't reach their ends.
Inputs may be any that keep to these rules, and one draw needn't show every extreme that they name: `expert_ids`: each token names 4 different experts. In each aligned block of 128 tokens (the tokens of one device) no expert is named by more than 10 tokens, a bound that some block reaches; every expert is named somewhere.
All inputs are finite; a program needn't handle non-finite values.
Results may differ from the reference program's by a relative error of at most 0.0064.
Values may be sent and summed in bfloat16 or wider, within the bound.
A program may use at most 32 MiB of HBM per device.

```python
import math
import jax
import jax.numpy as jnp
import numpy as np
from jax import lax

D = 8192
FF = 224
TOP = 4
TOK_DEV = 128
EXPERTS = 64
TOKENS = 16384
MOST = 10


def place_ends(array, key, smallest, largest):
    spot = [jax.random.randint(jax.random.fold_in(key, axis), (), 0, length) for axis, length in enumerate(array.shape)]
    widest = array.shape.index(max(array.shape))
    neighbour = spot[:widest] + [(spot[widest] + 1) % array.shape[widest]] + spot[widest + 1:]
    return array.at[tuple(spot)].set(smallest).at[tuple(neighbour)].set(largest)


def block_scale(key, shape, split, least, high):
    level, own = 1.0, jax.random.fold_in(key, 6)
    for position, shards_of in split:
        draws = jnp.exp(jax.random.uniform(jax.random.fold_in(own, position), (shards_of,), jnp.float32, least / len(split), high / len(split)))
        level = level * jnp.repeat(draws, shape[position] // shards_of).reshape([-1 if axis == position else 1 for axis in range(len(shape))])
    return level


def shared_out(own_key, own, number, rows, count, top, bound, slope):
    sequence = jax.random.permutation(own_key, count)
    packed, usual = portions_of(count, rows * top, bound, slope, True), portions_of(count, rows * top, bound, slope, False)
    places = jnp.arange(count)

    def named(lengths, rotation):
        used = int((lengths > 0).sum())
        fixed = max(1, used // 4)
        shifted = fixed + (places - fixed + rotation * (used - fixed)) % max(1, count - fixed)
        return jnp.zeros((count,), jnp.int32).at[sequence[jnp.where(places < fixed, places, shifted)]].set(jnp.asarray(lengths, jnp.int32))

    lengths = jnp.where(number % 4 == 0, named(packed, number // 4), named(usual, number - number // 4 - 1))
    mixed = jax.random.permutation(jax.random.fold_in(own, 3), count)
    source_of, taker = mixed[0:count // 2 * 2:2], mixed[1:count // 2 * 2:2]
    margin = jnp.minimum(lengths[source_of] - 1, bound - lengths[taker]) // 2
    margin = jnp.where((source_of == sequence[0]) | (taker == sequence[0]) | (lengths[taker] == 0), 0, jnp.maximum(margin, 0))
    shifted = jax.random.randint(jax.random.fold_in(own, 4), (count // 2,), 0, 1 << 20) % (margin + 1)
    lengths = lengths.at[source_of].add(-shifted).at[taker].add(shifted)
    items = jnp.searchsorted(jnp.cumsum(lengths), jnp.arange(rows * top), side="right").astype(jnp.int32)
    listing = items.reshape(top, rows).T
    listing = listing[jax.random.permutation(jax.random.fold_in(own, 1), rows)]
    rotation = jax.random.randint(jax.random.fold_in(own, 2), (rows, 1), 0, top)
    return jnp.take_along_axis(listing, (jnp.arange(top)[None, :] + rotation) % top, axis=1)


def portions_of(count, total, most, lean, full):
    loads = [(1 << 20) // math.isqrt(grade ** lean) + 1 for grade in range(1, count + 1)]
    largest = most if full else min(most, max(-(-total // count), total * loads[0] // sum(loads)))
    least = 1 if total - largest >= count - 1 else 0
    holding, spare = [largest] + [least] * (count - 1), total - largest - least * (count - 1)
    while spare > 0:
        free = [i for i in range(1, count) if holding[i] < largest] or [i for i in range(1, count) if holding[i] < most]
        mass, budget = sum([loads[i] for i in free]), spare
        for i in free:
            addition = min(most - holding[i], max(1, budget * loads[i] // mass), spare)
            holding[i] = holding[i] + addition
            spare = spare - addition
    return np.array(holding)


def normal_values(rng, dims, scale, most, pieces=(), held_as=jnp.bfloat16):
    drawn = scale * jax.random.normal(rng, dims, jnp.float32)
    if pieces:
        drawn = drawn * block_scale(rng, dims, pieces, -0.22, 0.18)
    return jnp.clip(drawn, -most, most).astype(held_as)


def setup_inputs(seed: int = 0) -> dict:
    seeds = jax.random.split(jax.random.key(seed), 7)
    tokens = normal_values(seeds[0], (TOKENS, D), 1.0, 6.0, ((0, 128), (1, 8)))
    cotangent = normal_values(seeds[1], (TOKENS, D), 1.0, 6.0, ((0, 128), (1, 8)))
    expert_ids_keys = jax.random.split(jax.random.fold_in(seeds[2], 1), TOKENS // TOK_DEV)
    expert_ids_turns = jax.random.permutation(jax.random.fold_in(seeds[2], 3), TOKENS // TOK_DEV)
    expert_ids = jax.vmap(lambda own, number: shared_out(jax.random.fold_in(seeds[2], 2), own, number, TOK_DEV, EXPERTS, TOP, MOST, 1))(expert_ids_keys, expert_ids_turns).reshape((TOKENS, TOP))
    gate_codes = place_ends(jax.random.randint(seeds[3], (TOKENS, TOP), 1, 256), jax.random.fold_in(seeds[3], 1), 1, 255).astype(jnp.int32)
    w_in = normal_values(seeds[4], (EXPERTS, D, 2 * FF), D ** -0.5, 0.0625, ((0, 32), (1, 8)))
    w_out = normal_values(seeds[5], (EXPERTS, FF, D), FF ** -0.5, 0.375, ((0, 32), (2, 8)))
    return {"tokens": tokens, "cotangent": cotangent, "expert_ids": expert_ids, "gate_codes": gate_codes, "w_in": w_in, "w_out": w_out}


def activate_grad(gate_up, hidden_grad, hidden_dim):
    gate_half = gate_up[..., :hidden_dim]
    up_half = gate_up[..., hidden_dim:]
    sigmoid_gate = jax.nn.sigmoid(gate_half)
    grad_gate = hidden_grad * up_half * sigmoid_gate * (1.0 + gate_half * (1.0 - sigmoid_gate))
    grad_up = hidden_grad * gate_half * sigmoid_gate
    return jnp.concatenate([grad_gate, grad_up], axis=-1).astype(jnp.bfloat16)

def reference(tokens, cotangent, expert_ids, gate_codes, w_in, w_out):
    route_count = TOKENS * TOP
    flat_ids = expert_ids.reshape(route_count)
    gate_values = gate_codes.astype(jnp.float32)
    route_weight = (gate_values / lax.optimization_barrier(jnp.sum(gate_values, axis=1, keepdims=True))).reshape(route_count)
    capacity = TOKENS // TOK_DEV * MOST

    def per_expert(total, expert):
        located = jnp.nonzero(flat_ids == expert, size=capacity, fill_value=route_count)[0].astype(jnp.int32)
        live_slot = located < route_count
        bounded = jnp.minimum(located, route_count - 1)
        token_index = bounded // TOP
        rows_in = jnp.where(live_slot[:, None], tokens[token_index], jnp.zeros((), jnp.bfloat16))
        scaled = route_weight[bounded][:, None] * cotangent[token_index].astype(jnp.float32)
        rows_grad = jnp.where(live_slot[:, None], scaled, 0.0).astype(jnp.bfloat16)
        weight_in = w_in[expert]
        weight_out = w_out[expert]
        gate_up = jnp.dot(rows_in, weight_in, preferred_element_type=jnp.float32)
        hidden_grad = jnp.dot(rows_grad, weight_out.T, preferred_element_type=jnp.float32)
        grad_gate_up = activate_grad(gate_up, hidden_grad, FF)
        route_grad = jnp.dot(grad_gate_up, weight_in.T, preferred_element_type=jnp.float32).astype(jnp.bfloat16)
        weight_grad = jnp.dot(rows_in.T, grad_gate_up, preferred_element_type=jnp.float32)
        added = jnp.where(live_slot[:, None], route_grad.astype(jnp.float32), 0.0)
        total = total.at[token_index].add(added)
        return (total, weight_grad)
    start = jnp.zeros((TOKENS, D), jnp.float32)
    total, grad_in = lax.scan(per_expert, start, jnp.arange(EXPERTS, dtype=jnp.int32))
    return (total.astype(jnp.bfloat16), grad_in)
```

```python
import functools

import jax
import jax.numpy as jnp
from jax import lax
from jax.experimental import pallas as pl
from jax.experimental.pallas import tpu as pltpu
from jax.sharding import PartitionSpec as P

MESH = pl.DeviceIdType.MESH
BF16, F32 = jnp.bfloat16, jnp.float32
TILE = 256


def dot(a, b):
    return jnp.dot(a, b, preferred_element_type=F32)


def dot_nt(a, b):
    return lax.dot_general(a, b, (((1,), (1,)), ((), ())), preferred_element_type=F32)


def dot_tn(a, b):
    return lax.dot_general(a, b, (((0,), (0,)), ((), ())), preferred_element_type=F32)


def kernel(
    cap, ring, cols, groups, stagger,
    ids_ref, codes_ref, tok_ref, cot_ref, win_ref, wout_ref,
    gtok_ref, gin_ref,
    aux, land_t, land_c, win4, wout4, pick, pick_t, slot_w, xt, xc,
    part_gu, part_h, recv_gu, recv_h, gg, rg, contrib, first, rs_r, rs_l,
    peer_x, peer_g, dp_out, dp_in,
    s_loc, s_peer, r_peer, s_aux, r_aux, s_ag, r_ag, s_gu, r_gu, s_h, r_h, s_gg, r_gg, s_rs, r_rs, s_dp, r_dp, go,
):
    T, D = tok_ref.shape
    F = wout_ref.shape[1]
    half = ring // 2
    NB = half
    UR = cap * NB
    R2 = 4 * UR
    R = 2 * R2
    QR = R // cols
    CH = 2
    TC = T // CH
    tile = min(TILE, D)
    me = lax.axis_index("expert")
    z, core = me // 2, me % 2
    my_q = lax.axis_index("col")
    my_g = lax.axis_index("dp")
    right = {"expert": lax.rem(me + 2, 2 * ring)}
    left = {"expert": lax.rem(me + 2 * ring - 2, 2 * ring)}
    mate = {"expert": me + 1 - 2 * core}
    cols_at = [{"col": lax.rem(my_q + d, cols)} for d in range(cols)]
    groups_at = [{"dp": lax.rem(my_g + d, groups)} for d in range(groups)]
    ways = (right, left)

    partners = [right, left, mate] + cols_at[1:] + groups_at[1:]
    barrier = pltpu.get_barrier_semaphore()
    for other in partners:
        pl.semaphore_signal(barrier, inc=1, device_id=other, device_id_type=MESH)
    pl.semaphore_wait(barrier, len(partners))

    sent = []

    def push(src, dst, send_sem, recv_sem, where):
        copy = pltpu.make_async_remote_copy(
            src_ref=src, dst_ref=dst, send_sem=send_sem, recv_sem=recv_sem, device_id=where, device_id_type=MESH
        )
        copy.start()
        sent.append(copy)
        return copy

    mine = pl.ds(2 * core, 2)
    local = [
        pltpu.make_async_copy(win_ref, win4.at[mine], s_loc.at[0]),
        pltpu.make_async_copy(wout_ref, wout4.at[mine], s_loc.at[1]),
    ]
    for copy in local:
        copy.start()
    w_in_copy = push(win_ref, win4.at[mine], s_peer.at[0], r_peer.at[0], mate)
    w_out_copy = push(wout_ref, wout4.at[mine], s_peer.at[1], r_peer.at[1], mate)

    codes = codes_ref[...].astype(F32)
    aux[0, 0:4, :] = ids_ref[...].astype(F32)
    aux[0, 4:8, :] = codes / jnp.sum(codes, axis=0, keepdims=True)
    land_t[0:T, :] = tok_ref[...]
    land_c[0:T, :] = cot_ref[...]

    if stagger:
        @pl.when(core == 1)
        def _():
            pl.semaphore_wait(go, 1)

    def place(way, k):
        if k == 0:
            return 0
        if k == half:
            return 2 * half - 1
        return 2 * k if way == 0 else 2 * k - 1

    land = (land_t, land_c)
    ag = {}
    aux_copy = {}

    def carries(way, k, c):
        return k < half or c == way

    def pass_on(arr, way, k, c):
        if k > half or not carries(way, k, c):
            return
        src = land[arr].at[pl.ds(place(way, k - 1) * T + c * TC, TC)]
        dst = land[arr].at[pl.ds(place(way, k) * T + c * TC, TC)]
        ag[arr, way, k, c] = push(src, dst, s_ag.at[arr, way, k - 1, c], r_ag.at[arr, way, k - 1, c], ways[way])

    def pass_aux(way, k):
        if k < half or (k == half and way == 0):
            aux_copy[way, k] = push(
                aux.at[place(way, k - 1)], aux.at[place(way, k)],
                s_aux.at[way, k - 1], r_aux.at[way, k - 1], ways[way],
            )

    def arrived(arr, k):
        for c in range(CH):
            for way in range(2):
                if (arr, way, k, c) in ag:
                    ag[arr, way, k, c].wait_recv()
                    pass_on(arr, way, k + 1, c)
        if arr == 0:
            for way in range(2):
                if (way, k) in aux_copy:
                    aux_copy[way, k].wait_recv()
                    pass_aux(way, k + 1)

    before = (lax.broadcasted_iota(jnp.int32, (T, T), 0) < lax.broadcasted_iota(jnp.int32, (T, T), 1)).astype(F32).astype(BF16)
    block_of = lax.broadcasted_iota(jnp.int32, (NB, T), 0)

    def build_pick(h):
        info = aux[h * NB:(h + 1) * NB]
        ids = [info[:, k, :] for k in range(4)]
        weights = [info[:, 4 + k, :] for k in range(4)]
        member, weight = [], []
        for e in range(4):
            number = (4 * z + e).astype(F32)
            hits = [ids[k] == number for k in range(4)]
            member.append(sum(jnp.where(hit, 1.0, 0.0) for hit in hits))
            weight.append(sum(jnp.where(hits[k], weights[k], 0.0) for k in range(4)))
        order = dot(jnp.concatenate(member, axis=0).astype(BF16), before)
        chosen, rows_w = [], []
        for e in range(4):
            at = order[e * NB:(e + 1) * NB]
            for j in range(cap):
                one = jnp.where(at == float(j), member[e], 0.0)
                chosen.append(one)
                rows_w.append(jnp.sum(one * weight[e], axis=1, keepdims=True))
        slot_w[h] = jnp.broadcast_to(jnp.concatenate(rows_w, axis=0), (R2, 128))
        for i in range(NB):
            rows = jnp.concatenate([jnp.where(block_of == i, one, 0.0) for one in chosen], axis=0)
            pick[h, :, i * T:(i + 1) * T] = rows.astype(BF16)
            pick_t[h * NB + i] = rows.T.astype(BF16)

    def compact(arr, h):
        def body(n, carry):
            at = pl.ds(pl.multiple_of(n * tile, tile), tile)
            rows = dot(pick[h], land[arr][h * NB * T:(h + 1) * NB * T, at])
            if arr == 1:
                rows = rows * slot_w[h][:, 0:1]
            rows = rows.astype(BF16)
            for e in range(4):
                (xt, xc)[arr][e, h * UR:(h + 1) * UR, at] = rows[e * UR:(e + 1) * UR]
            return carry
        lax.fori_loop(0, D // tile, body, 0)

    def gate_up(e, carry):
        rows = pl.ds(pl.multiple_of(e * 2 * UR, 2 * UR), 2 * UR)
        part_gu[0, rows, :] = dot_nt(xt[e], win4[e, 0:F, :])
        part_gu[1, rows, :] = dot_nt(xt[e], win4[e, F:2 * F, :])
        return carry

    def hidden(e, carry):
        rows = pl.ds(pl.multiple_of(e * 2 * UR, 2 * UR), 2 * UR)
        part_h[rows, :] = dot_nt(xc[e], wout4[e])
        return carry

    def rows_of(d):
        return pl.ds(pl.multiple_of(lax.rem(my_q + d, cols) * QR, QR), QR)

    far_first = sorted(range(1, cols), key=lambda d: -min(d, cols - d))
    gu_copies, h_copies, gg_copies, peer_copies = [], [], [], []

    def send_gate_up():
        for copy in local:
            copy.wait()
        w_in_copy.wait_recv()
        w_out_copy.wait_recv()
        lax.fori_loop(0, 4, gate_up, 0)
        for d in far_first:
            gu_copies.append(push(part_gu.at[:, rows_of(d)], recv_gu.at[d - 1], s_gu.at[d - 1], r_gu.at[d - 1], cols_at[d]))
        peer_copies.append(push(xt.at[pl.ds(2 - 2 * core, 2)], peer_x, s_peer.at[2], r_peer.at[2], mate))

    tasks = [
        (0, half // 2, lambda: build_pick(0)),
        (0, half // 2 + 1, lambda: compact(0, 0)),
        (1, 1, lambda: build_pick(1)),
        (1, 2, lambda: compact(0, 1)),
        (1, 3, send_gate_up),
        (1, half // 2 + 1, lambda: compact(1, 0)),
    ]

    def work(arr, k):
        if tasks and (tasks[0][0], tasks[0][1]) <= (arr, k):
            tasks.pop(0)[2]()

    for way in range(2):
        pass_aux(way, 1)
    for arr in range(2):
        for c in range(CH):
            for way in range(2):
                pass_on(arr, way, 1, c)
        if arr == 1:
            arrived(0, half)
        for k in range(1, half):
            arrived(arr, k)
            work(arr, k)
    while tasks:
        work(2, 0)
    arrived(1, half)
    if stagger:
        pl.semaphore_signal(go, inc=1, device_id=mate, device_id_type=MESH)
    compact(1, 1)
    lax.fori_loop(0, 4, hidden, 0)
    for d in far_first:
        h_copies.append(push(part_h.at[rows_of(d)], recv_h.at[d - 1], s_h.at[d - 1], r_h.at[d - 1], cols_at[d]))

    own = rows_of(0)
    gate, up = part_gu[0, own, :], part_gu[1, own, :]
    for copy in gu_copies:
        copy.wait_recv()
    for d in range(cols - 1):
        gate = gate + recv_gu[d, 0]
        up = up + recv_gu[d, 1]
    s = jax.nn.sigmoid(gate)
    slope = up * s * (1.0 + gate * (1.0 - s))
    act = gate * s
    grad = part_h[own, :]
    for copy in h_copies:
        copy.wait_recv()
    for d in range(cols - 1):
        grad = grad + recv_h[d]
    gg[0, own, :] = (grad * slope).astype(BF16)
    gg[1, own, :] = (grad * act).astype(BF16)
    for d in far_first:
        gg_copies.append(push(gg.at[:, own], gg.at[:, own], s_gg.at[d - 1], r_gg.at[d - 1], cols_at[d]))
    for d in range(1, cols):
        pltpu.make_async_remote_copy(
            src_ref=gg.at[:, rows_of(cols - d)], dst_ref=gg.at[:, rows_of(cols - d)], send_sem=s_gg.at[d - 1],
            recv_sem=r_gg.at[d - 1], device_id=cols_at[d], device_id_type=MESH,
        ).wait_recv()
    theirs = pl.ds(pl.multiple_of((1 - core) * R2, R2), R2)
    peer_copies.append(push(gg.at[:, theirs], peer_g, s_peer.at[3], r_peer.at[3], mate))

    def route_grad(e, carry):
        rows = pl.ds(pl.multiple_of(e * 2 * UR, 2 * UR), 2 * UR)
        g0, g1 = gg[0, rows, :], gg[1, rows, :]
        at = pl.ds(pl.multiple_of(e * UR, UR), UR)

        def body(n, carry):
            lanes = pl.ds(pl.multiple_of(n * tile, tile), tile)
            both = (dot(g0, win4[e, 0:F, lanes]) + dot(g1, win4[e, F:2 * F, lanes])).astype(BF16)
            rg[0, at, lanes] = both[0:UR]
            rg[1, at, lanes] = both[UR:2 * UR]
            return carry
        return lax.fori_loop(0, D // tile, body, carry)

    lax.fori_loop(0, 4, route_grad, 0)

    def contribution(into, p):
        def body(n, carry):
            lanes = pl.ds(pl.multiple_of(n * tile, tile), tile)
            contrib[into, :, lanes] = dot(pick_t[p], rg[p // NB, :, lanes])
            return carry
        lax.fori_loop(0, D // tile, body, 0)

    share = D // groups

    def weight_grad(d):
        lanes = pl.ds(pl.multiple_of(lax.rem(my_g + d, groups) * share, share), share)
        for l in range(2):
            rows = pl.ds(pl.multiple_of((2 * core + l) * 2 * UR, 2 * UR), 2 * UR)
            x = jnp.concatenate([xt[2 * core + l, :, lanes], peer_x[l, :, lanes]], axis=0)
            for g in range(2):
                grads = jnp.concatenate([gg[g, rows, :], peer_g[g, l * 2 * UR:(l + 1) * 2 * UR, :]], axis=0)
                value = dot_tn(grads, x)
                if d == 0:
                    gin_ref[l, g * F:(g + 1) * F, :] = value
                else:
                    dp_out[d - 1, l, g * F:(g + 1) * F, :] = value.astype(BF16)

    dp_copies = []

    def send_weight_grad(d):
        weight_grad(d)
        dp_copies.append(push(dp_out.at[d - 1], dp_in.at[d - 1], s_dp.at[d - 1], r_dp.at[d - 1], groups_at[d]))

    def peers_ready():
        for copy in peer_copies:
            copy.wait_recv()

    later = [peers_ready]
    for d in sorted(range(1, groups), key=lambda d: -min(d, groups - d)):
        later.append(functools.partial(send_weight_grad, d))
    later.append(lambda: weight_grad(0))

    if stagger:
        @pl.when(core == 0)
        def _():
            pl.semaphore_wait(go, 1)
    rs = (rs_r, rs_l)
    rs_copy = {}

    def rs_send(way, k, c, src):
        rs_copy[way, k, c] = push(
            src, rs[way].at[k - 1, pl.ds(c * TC, TC)], s_rs.at[way, k - 1, c], r_rs.at[way, k - 1, c], ways[way]
        )

    contribution(0, 2 * half - 1)
    for way in range(2):
        first[way] = contrib[0, way * TC:(way + 1) * TC, :].astype(BF16)
        rs_send(way, 1, way, first.at[way])
    for k in range(2, half + 1):
        o = half + 1 - k
        for way in range(2):
            contribution(way, 2 * o - 1 + way)
        for c in range(CH):
            for way in range(2):
                at = pl.ds(c * TC, TC)
                total = contrib[way, c * TC:(c + 1) * TC, :]
                if (way, k - 1, c) in rs_copy:
                    rs_copy[way, k - 1, c].wait_recv()
                    total = total + rs[way][k - 2, c * TC:(c + 1) * TC, :].astype(F32)
                rs[way][k - 2, c * TC:(c + 1) * TC, :] = total.astype(BF16)
                rs_send(way, k, c, rs[way].at[k - 2, at])
        if later:
            later.pop(0)()
    while later:
        later.pop(0)()
    contribution(0, 0)
    for c in range(CH):
        at = slice(c * TC, (c + 1) * TC)
        total = contrib[0, at, :]
        for way in range(2):
            rs_copy[way, half, c].wait_recv()
            total = total + rs[way][half - 1, at, :].astype(F32)
        gtok_ref[at, :] = total.astype(BF16)
    for copy in dp_copies:
        copy.wait_recv()
    for l in range(2):
        total = gin_ref[l]
        for d in range(groups - 1):
            total = total + dp_in[d, l].astype(F32)
        gin_ref[l] = total
    for copy in sent:
        copy.wait_send()


def per_device(stagger, tokens, cotangent, expert_ids, gate_codes, w_in, w_out):
    T, D = tokens.shape
    top = expert_ids.shape[1]
    F = w_out.shape[1]
    owners, cols, groups = lax.axis_size("expert"), lax.axis_size("col"), lax.axis_size("dp")
    ring = owners // 2
    half = ring // 2
    experts = w_in.shape[0] * owners
    cap = T * top // experts * 5 // 4
    UR = cap * half
    R2, R = 4 * UR, 8 * UR
    QR = R // cols
    share = D // groups
    V = pltpu.VMEM
    DMA = pltpu.SemaphoreType.DMA
    scratch = [
        V((ring, 8, T), F32),
        V((ring * T, D), BF16), V((ring * T, D), BF16),
        V((4, 2 * F, D), BF16), V((4, F, D), BF16),
        V((2, R2, half * T), BF16), V((ring, T, R2), BF16), V((2, R2, 128), F32),
        V((4, 2 * UR, D), BF16), V((4, 2 * UR, D), BF16),
        V((2, R, F), F32), V((R, F), F32),
        V((max(1, cols - 1), 2, QR, F), F32), V((max(1, cols - 1), QR, F), F32),
        V((2, R, F), BF16), V((2, R2, D), BF16), V((2, T, D), F32),
        V((2, T // 2, D), BF16), V((half, T, D), BF16), V((half, T, D), BF16),
        V((2, 2 * UR, D), BF16), V((2, R2, F), BF16),
        V((max(1, groups - 1), 2, 2 * F, share), BF16), V((max(1, groups - 1), 2, 2 * F, share), BF16),
        DMA((2,)), DMA((4,)), DMA((4,)),
        DMA((2, half)), DMA((2, half)),
        DMA((2, 2, half, 2)), DMA((2, 2, half, 2)),
        DMA((cols,)), DMA((cols,)), DMA((cols,)), DMA((cols,)), DMA((cols,)), DMA((cols,)),
        DMA((2, half, 2)), DMA((2, half, 2)),
        DMA((groups,)), DMA((groups,)),
        pltpu.SemaphoreType.REGULAR,
    ]
    vmem = pl.BlockSpec(memory_space=pltpu.VMEM)
    grad_tokens, grad_in = pl.pallas_call(
        functools.partial(kernel, cap, ring, cols, groups, stagger),
        out_shape=(jax.ShapeDtypeStruct((T, D), BF16), jax.ShapeDtypeStruct((2, 2 * F, share), F32)),
        in_specs=[vmem, vmem, vmem, vmem, pl.BlockSpec(memory_space=pl.ANY), pl.BlockSpec(memory_space=pl.ANY)],
        out_specs=(vmem, vmem),
        scratch_shapes=scratch,
        compiler_params=pltpu.CompilerParams(
            collective_id=0, has_side_effects=True, vmem_limit_bytes=56 * 1024 * 1024
        ),
        cost_estimate=pl.CostEstimate(flops=10**10, bytes_accessed=10**7, transcendentals=10**5),
    )(expert_ids.T, gate_codes.T, tokens, cotangent, jnp.swapaxes(w_in, 1, 2), w_out)
    return grad_tokens, jnp.swapaxes(grad_in, 1, 2)


def solution(mesh):
    placed = (
        P(("expert", "dp"), "col"),
        P(("expert", "dp"), "col"),
        P(("expert", "dp"), None),
        P(("expert", "dp"), None),
        P("expert", "col", None),
        P("expert", None, "col"),
    )
    return jax.shard_map(
        functools.partial(per_device, STAGGER),
        mesh=mesh,
        in_specs=placed,
        out_specs=(P(("expert", "dp"), "col"), P("expert", ("col", "dp"), None)),
        check_vma=False,
    )


STAGGER = False
```

```python
import functools

import jax
import jax.numpy as jnp
from jax import lax
from jax.experimental import pallas as pl
from jax.experimental.pallas import tpu as pltpu
from jax.sharding import PartitionSpec as P

MESH = pl.DeviceIdType.MESH
BF16, F32 = jnp.bfloat16, jnp.float32
TILE = 256


def dot(a, b):
    return jnp.dot(a, b, preferred_element_type=F32)


def dot_nt(a, b):
    return lax.dot_general(a, b, (((1,), (1,)), ((), ())), preferred_element_type=F32)


def dot_tn(a, b):
    return lax.dot_general(a, b, (((0,), (0,)), ((), ())), preferred_element_type=F32)


def kernel(
    cap, ring, cols, groups, plan,
    ids_ref, codes_ref, tok_ref, cot_ref, win_ref, wout_ref,
    gtok_ref, gin_ref,
    aux, land_t, land_c, win4, wout4, pick, pick_t, slot_w, xt, xc,
    part_gu, part_h, recv_gu, recv_h, sa, hh, gg, rg, contrib, rs_f, rs_r, rs_l,
    peer_x, peer_g, dp_out, dp_in,
    s_loc, s_peer, r_peer, s_aux, r_aux, s_ag, r_ag, s_gu, r_gu, s_h, r_h, s_sa, r_sa, s_hh, r_hh, s_rs, r_rs, s_dp, r_dp, go,
):
    T, D = tok_ref.shape
    F = wout_ref.shape[1]
    half = ring // 2
    NB = half
    UR = cap * NB
    R2 = 4 * UR
    R = 2 * R2
    QR = R // cols
    CH = plan["gather_chunks"]
    TC = T // CH
    RC = plan["return_chunks"]
    TR = T // RC
    lead = plan["lead"]
    tile = min(TILE, D)
    me = lax.axis_index("expert")
    z, core = me // 2, me % 2
    my_q = lax.axis_index("col")
    my_g = lax.axis_index("dp")
    right = {"expert": lax.rem(me + 2, 2 * ring)}
    left = {"expert": lax.rem(me + 2 * ring - 2, 2 * ring)}
    mate = {"expert": me + 1 - 2 * core}
    cols_at = [{"col": lax.rem(my_q + d, cols)} for d in range(cols)]
    groups_at = [{"dp": lax.rem(my_g + d, groups)} for d in range(groups)]
    ways = (right, left)

    partners = [right, left, mate] + cols_at[1:] + groups_at[1:]
    barrier = pltpu.get_barrier_semaphore()
    for other in partners:
        pl.semaphore_signal(barrier, inc=1, device_id=other, device_id_type=MESH)
    pl.semaphore_wait(barrier, len(partners))

    sent = []

    def ready(src, dst, send_sem, recv_sem, where):
        copy = pltpu.make_async_remote_copy(
            src_ref=src, dst_ref=dst, send_sem=send_sem, recv_sem=recv_sem, device_id=where, device_id_type=MESH
        )
        sent.append(copy)
        return copy

    def push(*copy):
        copy = ready(*copy)
        copy.start()
        return copy

    mine = pl.ds(2 * core, 2)
    local = [
        pltpu.make_async_copy(win_ref, win4.at[mine], s_loc.at[0]),
        pltpu.make_async_copy(wout_ref, wout4.at[mine], s_loc.at[1]),
    ]
    for copy in local:
        copy.start()
    w_in_copy = push(win_ref, win4.at[mine], s_peer.at[0], r_peer.at[0], mate)
    w_out_copy = push(wout_ref, wout4.at[mine], s_peer.at[1], r_peer.at[1], mate)

    codes = codes_ref[...].astype(F32)
    aux[0, 0:4, :] = ids_ref[...].astype(F32)
    aux[0, 4:8, :] = codes / jnp.sum(codes, axis=0, keepdims=True)
    land_t[0:T, :] = tok_ref[...]
    land_c[0:T, :] = cot_ref[...]

    if lead:
        @pl.when(core == 1)
        def _():
            pl.semaphore_wait(go.at[0], 1)

    def place(way, k):
        if k == 0:
            return 0
        if k == half:
            return 2 * half - 1
        return 2 * k if way == 0 else 2 * k - 1

    land = (land_t, land_c)
    ag = {}
    aux_copy = {}

    def carries(way, k, c):
        return k < half or c // (CH // 2) == way

    def pass_on(arr, way, k, c):
        if k > half or not carries(way, k, c):
            return
        src = land[arr].at[pl.ds(place(way, k - 1) * T + c * TC, TC)]
        dst = land[arr].at[pl.ds(place(way, k) * T + c * TC, TC)]
        ag[arr, way, k, c] = push(src, dst, s_ag.at[arr, way, k - 1, c], r_ag.at[arr, way, k - 1, c], ways[way])

    def pass_aux(way, k):
        if k < half or (k == half and way == 0):
            aux_copy[way, k] = push(
                aux.at[place(way, k - 1)], aux.at[place(way, k)],
                s_aux.at[way, k - 1], r_aux.at[way, k - 1], ways[way],
            )

    def arrived(arr, k):
        if lead:
            for turn, at in enumerate((lead, plan["release"])):
                if (arr, k) == at:
                    pl.semaphore_signal(go.at[turn], inc=1, device_id=mate, device_id_type=MESH)
        for c in range(CH):
            for way in range(2):
                if (arr, way, k, c) in ag:
                    ag[arr, way, k, c].wait_recv()
                    pass_on(arr, way, k + 1, c)
            if c == 0 and arr == 0:
                for way in range(2):
                    if (way, k) in aux_copy:
                        aux_copy[way, k].wait_recv()
                        pass_aux(way, k + 1)
            if k < half:
                work(arr, k if c == CH - 1 else k - 1)

    before = (lax.broadcasted_iota(jnp.int32, (T, T), 0) < lax.broadcasted_iota(jnp.int32, (T, T), 1)).astype(F32).astype(BF16)
    block_of = lax.broadcasted_iota(jnp.int32, (NB, T), 0)

    def build_pick(h):
        info = aux[h * NB:(h + 1) * NB]
        ids = [info[:, k, :] for k in range(4)]
        weights = [info[:, 4 + k, :] for k in range(4)]
        member, weight = [], []
        for e in range(4):
            number = (4 * z + e).astype(F32)
            hits = [ids[k] == number for k in range(4)]
            member.append(sum(jnp.where(hit, 1.0, 0.0) for hit in hits))
            weight.append(sum(jnp.where(hits[k], weights[k], 0.0) for k in range(4)))
        order = dot(jnp.concatenate(member, axis=0).astype(BF16), before)
        chosen, rows_w = [], []
        for e in range(4):
            at = order[e * NB:(e + 1) * NB]
            for j in range(cap):
                one = jnp.where(at == float(j), member[e], 0.0)
                chosen.append(one)
                rows_w.append(jnp.sum(one * weight[e], axis=1, keepdims=True))
        slot_w[h] = jnp.broadcast_to(jnp.concatenate(rows_w, axis=0), (R2, 128))
        for i in range(NB):
            rows = jnp.concatenate([jnp.where(block_of == i, one, 0.0) for one in chosen], axis=0)
            pick[h, :, i * T:(i + 1) * T] = rows.astype(BF16)
            pick_t[(h * NB + i) * T:(h * NB + i + 1) * T, :] = rows.T.astype(BF16)

    def compact(arr, h, lo, hi):
        def body(n, carry):
            at = pl.ds(pl.multiple_of(n * tile, tile), tile)
            rows = dot(pick[h], land[arr][h * NB * T:(h + 1) * NB * T, at])
            if arr == 1:
                rows = rows * slot_w[h][:, 0:1]
            rows = rows.astype(BF16)
            for e in range(4):
                (xt, xc)[arr][e, h * UR:(h + 1) * UR, at] = rows[e * UR:(e + 1) * UR]
            return carry
        lax.fori_loop(lo * (D // tile) // 2, hi * (D // tile) // 2, body, 0)

    def rows_at(e, h):
        return pl.ds(pl.multiple_of(e * 2 * UR + h * UR, UR), UR)

    def gate_up(h, lo):
        def body(e, carry):
            x = xt[e, h * UR:(h + 1) * UR, :]
            part_gu[0, rows_at(e, h), :] = dot_nt(x, win4[e, 0:F, :])
            part_gu[1, rows_at(e, h), :] = dot_nt(x, win4[e, F:2 * F, :])
            return carry
        lax.fori_loop(lo, lo + 2, body, 0)

    def hidden(h):
        def body(e, carry):
            part_h[rows_at(e, h), :] = dot_nt(xc[e, h * UR:(h + 1) * UR, :], wout4[e]).astype(BF16)
            return carry
        lax.fori_loop(0, 4, body, 0)

    split = QR == UR

    def rows_of(d):
        return pl.ds(pl.multiple_of(lax.rem(my_q + d, cols) * QR, QR), QR)

    def in_half(d, h):
        return lax.rem(lax.rem(my_q + d, cols), 2) == h

    def when_half(d, h, fn):
        if split:
            pl.when(in_half(d, h))(fn)
        elif h == 1:
            fn()

    far_first = sorted(range(1, cols), key=lambda d: -min(d, cols - d))
    peer_copies = []
    gu_copies = {d: ready(part_gu.at[:, rows_of(d)], recv_gu.at[d - 1], s_gu.at[d - 1], r_gu.at[d - 1], cols_at[d]) for d in far_first}
    h_copies = {d: ready(part_h.at[rows_of(d)], recv_h.at[d - 1], s_h.at[d - 1], r_h.at[d - 1], cols_at[d]) for d in far_first}
    hh_copies = {d: ready(hh.at[rows_of(0)], hh.at[rows_of(0)], s_hh.at[d - 1], r_hh.at[d - 1], cols_at[d]) for d in far_first}
    sa_copies = {d: ready(sa.at[:, rows_of(0)], sa.at[:, rows_of(0)], s_sa.at[d - 1], r_sa.at[d - 1], cols_at[d]) for d in far_first}

    def weights_ready():
        for copy in local:
            copy.wait()
        w_in_copy.wait_recv()
        w_out_copy.wait_recv()

    def send_gate_up(h):
        for d in far_first:
            when_half(d, h, gu_copies[d].start)
        if h == 1:
            peer_copies.append(push(xt.at[pl.ds(2 - 2 * core, 2)], peer_x, s_peer.at[2], r_peer.at[2], mate))

    def send_hidden(h):
        for d in far_first:
            when_half(d, h, h_copies[d].start)

    def share_slopes():
        own = rows_of(0)
        gate, up = part_gu[0, own, :], part_gu[1, own, :]
        for d in range(1, cols):
            gu_copies[d].wait_recv()
        for d in range(cols - 1):
            gate = gate + recv_gu[d, 0]
            up = up + recv_gu[d, 1]
        s = jax.nn.sigmoid(gate)
        sa[0, own, :] = (up * s * (1.0 + gate * (1.0 - s))).astype(BF16)
        sa[1, own, :] = (gate * s).astype(BF16)
        for d in far_first:
            sa_copies[d].start()

    def share_hidden():
        own = rows_of(0)
        grad = part_h[own, :].astype(F32)
        for d in range(1, cols):
            h_copies[d].wait_recv()
        for d in range(cols - 1):
            grad = grad + recv_h[d].astype(F32)
        hh[own, :] = grad.astype(BF16)
        for d in far_first:
            hh_copies[d].start()

    def landing(ref, sems, d):
        where = ref.at[rows_of(cols - d)] if len(ref.shape) == 2 else ref.at[:, rows_of(cols - d)]
        return pltpu.make_async_remote_copy(
            src_ref=where, dst_ref=where, send_sem=sems[0].at[d - 1], recv_sem=sems[1].at[d - 1],
            device_id=cols_at[d], device_id_type=MESH,
        )

    def slopes_here():
        for d in range(1, cols):
            landing(sa, (s_sa, r_sa), d).wait_recv()

    def hidden_here(h):
        for d in range(1, cols):
            when_half(cols - d, h, landing(hh, (s_hh, r_hh), d).wait_recv)

    tasks = [
        (0, half // 2, lambda: build_pick(0)),
        (0, half // 2 + 1, lambda: compact(0, 0, 0, 1)),
        (0, half // 2 + 1, lambda: compact(0, 0, 1, 2)),
        (0, half // 2 + 1, weights_ready),
        (0, half // 2 + 1, lambda: gate_up(0, 0)),
        (0, half // 2 + 1, lambda: gate_up(0, 2)),
        (0, half // 2 + 1, lambda: send_gate_up(0)),
        (1, 1, lambda: build_pick(1)),
        (1, 1, lambda: compact(0, 1, 0, 1)),
        (1, 1, lambda: compact(0, 1, 1, 2)),
        (1, 1, lambda: gate_up(1, 0)),
        (1, 1, lambda: gate_up(1, 2)),
        (1, 1, lambda: send_gate_up(1)),
        (1, half // 2, lambda: compact(1, 0, 0, 1)),
        (1, half // 2, lambda: compact(1, 0, 1, 2)),
        (1, half // 2, lambda: hidden(0)),
        (1, half // 2, lambda: send_hidden(0)),
        (1, half - 2, share_slopes),
    ]
    if split:
        tasks.append((1, half - 1, lambda: pl.when(in_half(0, 0))(share_hidden)))

    def work(arr, k):
        if tasks and (tasks[0][0], tasks[0][1]) <= (arr, k):
            tasks.pop(0)[2]()

    for way in range(2):
        pass_aux(way, 1)
    for arr in range(2):
        for c in range(CH):
            for way in range(2):
                pass_on(arr, way, 1, c)
        if arr == 1:
            arrived(0, half)
        for k in range(1, half):
            arrived(arr, k)
    while tasks:
        work(2, 0)
    arrived(1, half)
    compact(1, 1, 0, 2)
    hidden(1)
    send_hidden(1)
    slopes_here()

    def route_grad(h):
        def body(e, carry):
            rows = rows_at(e, h)
            grad = hh[rows, :].astype(F32)
            g0 = (grad * sa[0, rows, :].astype(F32)).astype(BF16)
            g1 = (grad * sa[1, rows, :].astype(F32)).astype(BF16)
            gg[0, rows, :] = g0
            gg[1, rows, :] = g1
            at = pl.ds(pl.multiple_of(e * UR, UR), UR)
            rg[h, at, :] = (dot(g0, win4[e, 0:F, :]) + dot(g1, win4[e, F:2 * F, :])).astype(BF16)
            return carry
        lax.fori_loop(0, 4, body, 0)

    if split:
        hidden_here(0)
        route_grad(0)
        pl.when(in_half(0, 1))(share_hidden)
        hidden_here(1)
    else:
        share_hidden()
        hidden_here(1)
        route_grad(0)
    route_grad(1)
    theirs = pl.ds(pl.multiple_of((1 - core) * R2, R2), R2)
    peer_copies.append(push(gg.at[:, theirs], peer_g, s_peer.at[3], r_peer.at[3], mate))

    def contributions(h):
        rows = slice(h * NB * T, (h + 1) * NB * T)

        def body(n, carry):
            lanes = pl.ds(pl.multiple_of(n * tile, tile), tile)
            contrib[rows, lanes] = dot(pick_t[rows], rg[h, :, lanes])
            return carry
        lax.fori_loop(0, D // tile, body, 0)

    share = D // groups

    def weight_grad(d):
        lanes = pl.ds(pl.multiple_of(lax.rem(my_g + d, groups) * share, share), share)
        for l in range(2):
            rows = pl.ds(pl.multiple_of((2 * core + l) * 2 * UR, 2 * UR), 2 * UR)
            x = jnp.concatenate([xt[2 * core + l, :, lanes], peer_x[l, :, lanes]], axis=0)
            for g in range(2):
                grads = jnp.concatenate([gg[g, rows, :], peer_g[g, l * 2 * UR:(l + 1) * 2 * UR, :]], axis=0)
                value = dot_tn(grads, x)
                if d == 0:
                    gin_ref[l, g * F:(g + 1) * F, :] = value
                else:
                    dp_out[d - 1, l, g * F:(g + 1) * F, :] = value.astype(BF16)

    dp_copies = []

    def send_weight_grad(d):
        weight_grad(d)
        dp_copies.append(push(dp_out.at[d - 1], dp_in.at[d - 1], s_dp.at[d - 1], r_dp.at[d - 1], groups_at[d]))

    def peers_ready():
        for copy in peer_copies:
            copy.wait_recv()

    later = [lambda: contributions(0), peers_ready]
    for d in sorted(range(1, groups), key=lambda d: -min(d, groups - d)):
        later.append(functools.partial(send_weight_grad, d))
    later.append(lambda: weight_grad(0))

    contributions(1)
    if lead:
        pl.semaphore_wait(go.at[1], 1)

        @pl.when(core == 0)
        def _():
            pl.semaphore_wait(go.at[0], 1)
    rs = (rs_r, rs_l)
    rs_copy = {}

    def rs_send(way, k, c, src):
        rs_copy[way, k, c] = push(
            src, rs[way].at[k - 1, pl.ds(c * TR, TR)], s_rs.at[way, k - 1, c], r_rs.at[way, k - 1, c], ways[way]
        )

    for c in range(RC // 2):
        for way in range(2):
            cc = c + way * (RC // 2)
            at = (2 * half - 1) * T + cc * TR
            rs_f[cc * TR:(cc + 1) * TR, :] = contrib[at:at + TR, :].astype(BF16)
            rs_send(way, 1, cc, rs_f.at[pl.ds(cc * TR, TR)])
    if half < 4:
        later.pop(0)()
    for k in range(2, half + 1):
        o = half + 1 - k
        for c in range(RC):
            for way in range(2):
                at = (2 * o - 1 + way) * T + c * TR
                total = contrib[at:at + TR, :]
                if (way, k - 1, c) in rs_copy:
                    rs_copy[way, k - 1, c].wait_recv()
                    total = total + rs[way][k - 2, c * TR:(c + 1) * TR, :].astype(F32)
                rs[way][k - 2, c * TR:(c + 1) * TR, :] = total.astype(BF16)
                rs_send(way, k, c, rs[way].at[k - 2, pl.ds(c * TR, TR)])
        if later:
            later.pop(0)()
    while later:
        later.pop(0)()
    for c in range(RC):
        at = slice(c * TR, (c + 1) * TR)
        total = contrib[at, :]
        for way in range(2):
            rs_copy[way, half, c].wait_recv()
            total = total + rs[way][half - 1, at, :].astype(F32)
        gtok_ref[at, :] = total.astype(BF16)
    for copy in dp_copies:
        copy.wait_recv()
    for l in range(2):
        total = gin_ref[l]
        for d in range(groups - 1):
            total = total + dp_in[d, l].astype(F32)
        gin_ref[l] = total
    for copy in sent:
        copy.wait_send()


def per_device(plan, tokens, cotangent, expert_ids, gate_codes, w_in, w_out):
    T, D = tokens.shape
    top = expert_ids.shape[1]
    F = w_out.shape[1]
    owners, cols, groups = lax.axis_size("expert"), lax.axis_size("col"), lax.axis_size("dp")
    ring = owners // 2
    half = ring // 2
    experts = w_in.shape[0] * owners
    cap = T * top // experts * 5 // 4
    UR = cap * half
    R2, R = 4 * UR, 8 * UR
    QR = R // cols
    share = D // groups
    rc, gc = plan["return_chunks"], plan["gather_chunks"]
    V = pltpu.VMEM
    DMA = pltpu.SemaphoreType.DMA
    scratch = [
        V((ring, 8, T), F32),
        V((ring * T, D), BF16), V((ring * T, D), BF16),
        V((4, 2 * F, D), BF16), V((4, F, D), BF16),
        V((2, R2, half * T), BF16), V((ring * T, R2), BF16), V((2, R2, 128), F32),
        V((4, 2 * UR, D), BF16), V((4, 2 * UR, D), BF16),
        V((2, R, F), F32), V((R, F), BF16),
        V((max(1, cols - 1), 2, QR, F), F32), V((max(1, cols - 1), QR, F), BF16),
        V((2, R, F), BF16), V((R, F), BF16), V((2, R, F), BF16), V((2, R2, D), BF16), V((ring * T, D), F32),
        V((T, D), BF16), V((half, T, D), BF16), V((half, T, D), BF16),
        V((2, 2 * UR, D), BF16), V((2, R2, F), BF16),
        V((max(1, groups - 1), 2, 2 * F, share), BF16), V((max(1, groups - 1), 2, 2 * F, share), BF16),
        DMA((2,)), DMA((4,)), DMA((4,)),
        DMA((2, half)), DMA((2, half)),
        DMA((2, 2, half, gc)), DMA((2, 2, half, gc)),
        *[DMA((cols,))] * 8,
        DMA((2, half, rc)), DMA((2, half, rc)),
        DMA((groups,)), DMA((groups,)),
        pltpu.SemaphoreType.REGULAR((2,)),
    ]
    vmem = pl.BlockSpec(memory_space=pltpu.VMEM)
    grad_tokens, grad_in = pl.pallas_call(
        functools.partial(kernel, cap, ring, cols, groups, plan),
        out_shape=(jax.ShapeDtypeStruct((T, D), BF16), jax.ShapeDtypeStruct((2, 2 * F, share), F32)),
        in_specs=[vmem, vmem, vmem, vmem, pl.BlockSpec(memory_space=pl.ANY), pl.BlockSpec(memory_space=pl.ANY)],
        out_specs=(vmem, vmem),
        scratch_shapes=scratch,
        compiler_params=pltpu.CompilerParams(
            collective_id=0, has_side_effects=True, vmem_limit_bytes=56 * 1024 * 1024
        ),
        cost_estimate=pl.CostEstimate(flops=10**10, bytes_accessed=10**7, transcendentals=10**5),
    )(expert_ids.T, gate_codes.T, tokens, cotangent, jnp.swapaxes(w_in, 1, 2), w_out)
    return grad_tokens, jnp.swapaxes(grad_in, 1, 2)


def solution(mesh):
    placed = (
        P(("expert", "dp"), "col"),
        P(("expert", "dp"), "col"),
        P(("expert", "dp"), None),
        P(("expert", "dp"), None),
        P("expert", "col", None),
        P("expert", None, "col"),
    )
    return jax.shard_map(
        functools.partial(per_device, PLAN),
        mesh=mesh,
        in_specs=placed,
        out_specs=(P(("expert", "dp"), "col"), P("expert", ("col", "dp"), None)),
        check_vma=False,
    )


PLAN = {"lead": None, "release": (1, 6), "gather_chunks": 4, "return_chunks": 4}
```
